256 devices in a mesh: view: 16 (over z, core), tok: 16 (over y, x).
Axes of the slice: x: 4, y: 4, z: 8, core: 2. Of those that a mesh axis runs over, the one named last changes fastest.
Arguments:
- queries: bfloat16 [6144, 1024], P('tok'), may hold values from -42 to 42
- keys: bfloat16 [16384, 1024], P('view'), may hold values from -16 to 16
- values: bfloat16 [16384, 1024], P('view'), may hold values from -6 to 6
- grad_out: bfloat16 [6144, 1024], P('tok'), may hold values from -6 to 6
- lengths: int32 [16], P('view'), may hold values from 1 to 1024, 10240 in all
Outputs:
- query_grad: bfloat16 [6144, 1024], P(('tok', 'view'))
- key_grad: bfloat16 [16384, 1024], P(('view', 'tok'))
- value_grad: bfloat16 [16384, 1024], P(('view', 'tok'))
The draws below stay inside these ranges and needn't reach their ends.
Inputs may be any that keep to these rules, and one draw needn't show every extreme that they name: `lengths`: every view has at least one valid patch; some view has all 1024.
All inputs are finite; a program needn't handle non-finite values. No bound on the sum of `lengths` on one device may be relied on, other than what follows from the above.
Results may differ from the reference program's by a relative error of at most 0.019.
Values may be sent and summed in bfloat16 or wider, within the bound.
A program may use at most 128 MiB of HBM per device.

```python
import math
import jax
import jax.numpy as jnp
import numpy as np
from jax import lax

HEADS = 16
HEAD = 64
D = 1024
TQ_DEV = 384
PATCHES = 1024
VIEWS = 16
NQ = 6144
NK = 16384
N_TOK = 16


def draw_keys(key, part):
    key = jax.random.fold_in(key, 11)
    result = jnp.clip(jax.random.normal(key, (PATCHES * VIEWS, HEADS * HEAD), jnp.float32), -4.0, 4.0)
    return result.astype(jnp.bfloat16)


def draw_queries(key, part):
    key = jax.random.fold_in(key, 23)
    result = jnp.clip(jax.random.normal(key, (TQ_DEV * N_TOK, HEADS * HEAD), jnp.float32), -4.0, 4.0)
    return result.astype(jnp.bfloat16)


def level_of(rng, shape, split, least, high):
    level = 1.0
    for dim, parts in split:
        steps = jax.random.uniform(jax.random.fold_in(jax.random.fold_in(rng, 6), dim), (parts,), jnp.float32, least / len(split), high / len(split))
        level = level * jnp.repeat(jnp.exp(steps), shape[dim] // parts).reshape((-1,) + (1,) * (len(shape) - 1 - dim))
    return level


def length_profile(amount, total, reach, slope):
    portions = [(1 << 20) // math.isqrt(grade ** slope) + 1 for grade in range(2, amount + 1)]
    spare, given = total - reach - (amount - 1), [1] * (amount - 1)
    while spare > 0:
        free = [i for i in range(amount - 1) if given[i] < reach]
        pool, remaining = sum([portions[i] for i in free]), spare
        for i in free:
            more = min(reach - given[i], max(1, remaining * portions[i] // pool), spare)
            given[i] = given[i] + more
            spare = spare - more
    return np.array([reach] + given)


def uneven(own_key, count, total, reach, slope):
    if count == 2:
        one = jax.random.randint(own_key, (), max(1, total - reach), min(reach, total - 1) + 1)
        return jnp.stack([one, total - one])
    tallies = jnp.asarray(length_profile(count, total, reach, slope), jnp.int32)
    couples = (count - 1) // 2
    giver, taker = tallies[1:1 + 2 * couples:2], tallies[2:2 + 2 * couples:2]
    slack = jnp.minimum(giver - 1, reach - taker)
    shifted = jax.random.randint(jax.random.fold_in(own_key, 1), (couples,), 0, 1 << 20) % (slack + 1)
    tallies = tallies.at[1:1 + 2 * couples:2].set(giver - shifted).at[2:2 + 2 * couples:2].set(taker + shifted)
    return tallies[jax.random.permutation(jax.random.fold_in(own_key, 2), count)]


def gaussian(stream_key, shape, spread, reach, shards=(), held_as=jnp.bfloat16):
    values = jax.random.normal(stream_key, shape, jnp.float32) * spread
    if len(shards) > 0:
        values = level_of(stream_key, shape, shards, -0.22, 0.18) * values
    return jnp.clip(values, min=-reach, max=reach).astype(held_as)


def setup_inputs(seed: int = 0) -> dict:
    seeds = jax.random.split(jax.random.key(seed), 6)
    queries = draw_queries(jax.random.fold_in(seeds[5], 71), 0)
    keys = draw_keys(jax.random.fold_in(seeds[5], 71), 0)
    values = gaussian(seeds[2], (NK, D), 1.0, 6.0, ((0, 16),))
    grad_out = gaussian(seeds[3], (NQ, D), 1.0, 6.0, ((0, 16),))
    lengths = uneven(seeds[4], VIEWS, VIEWS * PATCHES * 5 // 8, PATCHES, 2).astype(jnp.int32)
    return dict(queries=queries, keys=keys, values=values, grad_out=grad_out, lengths=lengths)


def reference(queries, keys, values, grad_out, lengths):
    nq, width = queries.shape
    nk = keys.shape[0]
    heads = width // HEAD
    scale = HEAD ** -0.5
    position = jnp.arange(nk, dtype=jnp.int32) % PATCHES
    limit = jnp.repeat(lengths.astype(jnp.int32), PATCHES)
    valid = position < limit

    def split_heads(x, rows):
        return x.reshape(rows, heads, HEAD).transpose(1, 0, 2)

    def one_head(items):
        q_head, k_head, v_head, g_head = items
        scores = jnp.einsum("qd,kd->qk", q_head, k_head, preferred_element_type=jnp.float32) * scale
        scores = jnp.where(valid[None, :], scores, jnp.float32(-1e30))
        row_max = jnp.max(scores, axis=1, keepdims=True)
        weights = jnp.exp(scores - row_max)
        row_total = jnp.sum(weights, axis=1, keepdims=True)
        probs = weights / row_total
        dprobs = jnp.einsum("qd,kd->qk", g_head, v_head, preferred_element_type=jnp.float32)
        delta = jnp.sum(probs * dprobs, axis=1, keepdims=True)
        dscores = (probs * (dprobs - delta) * scale).astype(jnp.bfloat16)
        probs_low = probs.astype(jnp.bfloat16)
        dq = jnp.einsum("qk,kd->qd", dscores, k_head, preferred_element_type=jnp.float32)
        dk = jnp.einsum("qk,qd->kd", dscores, q_head, preferred_element_type=jnp.float32)
        dv = jnp.einsum("qk,qd->kd", probs_low, g_head, preferred_element_type=jnp.float32)
        return dq.astype(jnp.bfloat16), dk.astype(jnp.bfloat16), dv.astype(jnp.bfloat16)

    dq, dk, dv = lax.map(one_head, (split_heads(queries, nq), split_heads(keys, nk), split_heads(values, nk), split_heads(grad_out, nq)))
    query_grad = dq.transpose(1, 0, 2).reshape(nq, width)
    key_grad = dk.transpose(1, 0, 2).reshape(nk, width)
    value_grad = dv.transpose(1, 0, 2).reshape(nk, width)
    return query_grad, key_grad, value_grad
```

```python
import functools

import jax
import jax.numpy as jnp
from jax import lax
from jax.experimental import pallas as pl
from jax.experimental.pallas import tpu as pltpu
from jax.sharding import PartitionSpec as P

HEAD = 64
PAIR = 128
ROWS = 384
BLOCK = 2 * ROWS
KEYS = 1024
BOTH = 2 * KEYS
NZ = 8
NT = 16
SLOTS = 4
PIECE = ROWS // NZ
SMALL = PIECE // 2
OUT_KEYS = KEYS // NT
STEP1 = 256
STEP2 = 512
MESH = pl.DeviceIdType.MESH
BF = jnp.bfloat16
F32 = jnp.float32
NN = (((1,), (0,)), ((), ()))


def mm(a, b):
    return lax.dot_general(a, b, NN, preferred_element_type=F32)


def kernel(
    len_ref, q_hbm, g_hbm, k_hbm, v_hbm,
    dq_out, dk_out, dv_out,
    q_v, g_v, k_v, v_v, qt, gt, qg_buf, kv_buf, len_buf,
    k0, v0, kt, vt1, s_ref, w_buf, dkv, stats,
    dq_send, dq_recv, dq_red, dkv_send, dkv_recv, dkv_fin, kv_tiles, dq_tiles,
    load_sem, qg_ssem, qg_rsem, kv_ssem, kv_rsem, st_ssem, st_rsem,
    dq_ssem, dq_rsem, x_ssem, x_rsem, fin_ssem, fin_rsem,
):
    v = lax.axis_index("view")
    t = lax.axis_index("tok")
    z = v // 2
    core = v % 2
    y = t // 4
    par = (t + core) % 2
    mate = (2 * z + 1 - core, t)
    scale = HEAD ** -0.5

    pair_cols = pl.ds(pl.multiple_of(PAIR * (t // 2), PAIR), PAIR)
    loads = [
        pltpu.make_async_copy(k_hbm.at[:, pair_cols], k_v, load_sem.at[0]),
        pltpu.make_async_copy(v_hbm.at[:, pair_cols], v_v, load_sem.at[1]),
        pltpu.make_async_copy(q_hbm, q_v, load_sem.at[2]),
        pltpu.make_async_copy(g_hbm, g_v, load_sem.at[3]),
    ]
    for load in loads:
        load.start()

    barrier = pltpu.get_barrier_semaphore()

    def greet_tok(d, _):
        pl.semaphore_signal(barrier, inc=1, device_id=(v, (t + d) % NT), device_id_type=MESH)
        return 0

    def greet_z(d, _):
        pl.semaphore_signal(
            barrier, inc=1, device_id=(2 * ((z + d) % NZ) + core, t), device_id_type=MESH
        )
        return 0

    lax.fori_loop(1, NT, greet_tok, 0)
    lax.fori_loop(1, NZ, greet_z, 0)
    pl.semaphore_signal(barrier, inc=1, device_id=mate, device_id_type=MESH)

    length = len_ref[0]
    lane = lax.broadcasted_iota(jnp.int32, (1, PAIR), 1)
    left = lane < HEAD
    row = lax.broadcasted_iota(jnp.int32, (KEYS, 1), 0)
    loads[0].wait()
    loads[1].wait()
    even = t % 2 == 0
    k_f = k_v[...].astype(F32)
    v_f = v_v[...].astype(F32)
    k_left = jnp.where(even, k_f, pltpu.roll(k_f, HEAD, 1))
    v_right = jnp.where(even, pltpu.roll(v_f, HEAD, 1), v_f)
    kv = jnp.where(left, k_left, v_right)
    kv = jnp.where(row < length, kv, kv[0:1, :])
    kv_buf[core] = kv.astype(BF)
    len_buf[core] = jnp.full((8, PAIR), length, jnp.int32).astype(F32)

    loads[2].wait()
    loads[3].wait()
    pl.semaphore_wait(barrier, NT - 1 + NZ - 1 + 1)

    kv_copy = pltpu.make_async_remote_copy(
        src_ref=kv_buf.at[core], dst_ref=kv_buf.at[core],
        send_sem=kv_ssem.at[0], recv_sem=kv_rsem.at[0],
        device_id=mate, device_id_type=MESH,
    )
    len_copy = pltpu.make_async_remote_copy(
        src_ref=len_buf.at[core], dst_ref=len_buf.at[core],
        send_sem=kv_ssem.at[1], recv_sem=kv_rsem.at[1],
        device_id=mate, device_id_type=MESH,
    )
    kv_copy.start()
    len_copy.start()

    def qg_copy(which, pair):
        src, dst_rows = ((qt, 0), (gt, HEAD))[which]
        dest = 2 * pair + par
        my_y = t // 4
        my_half = (t // 2) % 2
        return pltpu.make_async_remote_copy(
            src_ref=src.at[pl.ds(pl.multiple_of(HEAD * dest, HEAD), HEAD), :],
            dst_ref=qg_buf.at[
                my_y, dst_rows : dst_rows + HEAD, pl.ds(pl.multiple_of(ROWS * my_half, ROWS), ROWS)
            ],
            send_sem=qg_ssem.at[which, pair],
            recv_sem=qg_rsem.at[which, t // 2],
            device_id=(v, dest),
            device_id_type=MESH,
        )

    def pack(j, _):
        pair = 2 * ((y + j // 2) % 4) + j % 2
        dest = 2 * pair + par
        cols = pl.ds(pl.multiple_of(PAIR * pair, PAIR), PAIR)
        qt[cols, :] = q_v[:, cols].T
        gt[cols, :] = g_v[:, cols].T

        @pl.when(dest != t)
        def _():
            qg_copy(0, pair).start()
            qg_copy(1, pair).start()

        @pl.when(dest == t)
        def _():
            here = pl.ds(pl.multiple_of(HEAD * dest, HEAD), HEAD)
            mine = pl.ds(pl.multiple_of(ROWS * ((t // 2) % 2), ROWS), ROWS)
            qg_buf[y, 0:HEAD, mine] = qt[here, :]
            qg_buf[y, HEAD:PAIR, mine] = gt[here, :]

        return 0

    lax.fori_loop(0, NT // 2, pack, 0)

    kv_copy.wait_recv()
    len_copy.wait_recv()
    col = lax.broadcasted_iota(jnp.int32, (1, KEYS), 1).astype(F32)
    sub = lax.broadcasted_iota(jnp.int32, (HEAD, 1), 0)
    for side in range(2):
        here = slice(side * KEYS, (side + 1) * KEYS)
        tile = kv_buf[side]
        f = tile.astype(F32)
        k0[here, :] = jnp.where(left, f, 0.0).astype(BF)
        v0[here, :] = jnp.where(left, 0.0, f).astype(BF)
        flipped = tile.T.astype(F32)
        okay = jnp.where(col < len_buf[side][0:1, 0:1], 1.0, 0.0)
        kt[:, here] = (flipped[0:HEAD] * okay).astype(BF)
        vt1[HEAD:PAIR, here] = (flipped[HEAD:PAIR] * okay).astype(BF)
        vt1[0:HEAD, here] = jnp.where(sub == 0, okay, 0.0).astype(BF)
    dkv[...] = jnp.zeros_like(dkv)

    def stat_copy(i, to):
        return pltpu.make_async_remote_copy(
            src_ref=stats.at[i, z], dst_ref=stats.at[i, z],
            send_sem=st_ssem.at[i, to], recv_sem=st_rsem.at[i, z],
            device_id=(2 * to + core, t), device_id_type=MESH,
        )

    def stat_arrival(i, frm):
        return pltpu.make_async_remote_copy(
            src_ref=stats.at[i, frm], dst_ref=stats.at[i, frm],
            send_sem=st_ssem.at[i, frm], recv_sem=st_rsem.at[i, frm],
            device_id=(2 * frm + core, t), device_id_type=MESH,
        )

    def dq_copy(i, to):
        return pltpu.make_async_remote_copy(
            src_ref=dq_send.at[i, pl.ds(pl.multiple_of(PIECE * to, PIECE), PIECE), :],
            dst_ref=dq_recv.at[i, z],
            send_sem=dq_ssem.at[i, to], recv_sem=dq_rsem.at[i, z],
            device_id=(2 * to + core, t), device_id_type=MESH,
        )

    def dq_arrival(i, frm):
        return pltpu.make_async_remote_copy(
            src_ref=dq_recv.at[i, frm], dst_ref=dq_recv.at[i, frm],
            send_sem=dq_ssem.at[i, frm], recv_sem=dq_rsem.at[i, frm],
            device_id=(2 * frm + core, t), device_id_type=MESH,
        )

    def block_of(i):
        return (y + 3 * i) % 4

    def scores_phase(i):
        sb = block_of(i)
        slot = i % 2
        for half in range(2):
            source = 4 * sb + 2 * half + par

            @pl.when(source != t)
            def _():
                for which in range(2):
                    pltpu.make_async_remote_copy(
                        src_ref=qt.at[0:HEAD, :],
                        dst_ref=qg_buf.at[
                            sb, which * HEAD : (which + 1) * HEAD, half * ROWS : (half + 1) * ROWS
                        ],
                        send_sem=qg_ssem.at[which, 2 * sb + half],
                        recv_sem=qg_rsem.at[which, 2 * sb + half],
                        device_id=(v, source),
                        device_id_type=MESH,
                    ).wait_recv()

        qg = qg_buf[sb]
        top = jnp.full((8, BLOCK), -3e38, F32)
        for k in range(BOTH // STEP1):
            here = slice(k * STEP1, (k + 1) * STEP1)
            s = mm(k0[here, :], qg)
            s_ref[here, :] = s
            top = jnp.maximum(top, jnp.max(s.reshape(STEP1 // 8, 8, BLOCK), axis=0))
        top = jnp.max(top, axis=0, keepdims=True)
        acc = jnp.zeros((PAIR, BLOCK), F32)
        for k in range(BOTH // STEP1):
            here = slice(k * STEP1, (k + 1) * STEP1)
            w = jnp.exp((s_ref[here, :] - top) * scale).astype(BF)
            w_buf[slot, here, :] = w
            acc = acc + mm(vt1[:, here], w)
        total = acc[0:1, :]
        mean = jnp.sum(acc[HEAD:, :] * qg[HEAD:, :].astype(F32), axis=0, keepdims=True)
        top = top * scale
        mine = stats.at[i, z]
        mine[0:1, :] = top[:, :ROWS]
        mine[1:2, :] = top[:, ROWS:]
        mine[2:3, :] = total[:, :ROWS]
        mine[3:4, :] = total[:, ROWS:]
        mine[4:5, :] = mean[:, :ROWS]
        mine[5:6, :] = mean[:, ROWS:]
        mine[6:8, :] = jnp.zeros((2, ROWS), F32)

        def send(d, _):
            stat_copy(i, (z + d) % NZ).start()
            return 0

        lax.fori_loop(1, NZ, send, 0)

    def grads_phase(i):
        sb = block_of(i)
        slot = i % 2

        def arrive(d, _):
            stat_arrival(i, (z + d) % NZ).wait_recv()
            return 0

        lax.fori_loop(1, NZ, arrive, 0)
        every = stats[i]
        tops = every[:, 0:2, :]
        top = jnp.max(tops, axis=0)
        weight = jnp.exp(tops - top[None])
        total = jnp.sum(every[:, 2:4, :] * weight, axis=0)
        mean = jnp.sum(every[:, 4:6, :] * weight, axis=0) / total
        factor = jnp.exp(stats[i, z, 0:2, :] - top) / total
        mean = jnp.concatenate([mean[0:1], mean[1:2]], axis=1)
        factor = jnp.concatenate([factor[0:1], factor[1:2]], axis=1)

        qg = qg_buf[sb]
        scaled = (qg.astype(F32) * factor).T
        cq = jnp.where(left, scaled * scale, 0.0).astype(BF)
        cg = jnp.where(left, 0.0, scaled).astype(BF)
        acc = jnp.zeros((HEAD, BLOCK), F32)
        for k in range(BOTH // STEP2):
            here = slice(k * STEP2, (k + 1) * STEP2)
            dp = mm(v0[here, :], qg)
            w = w_buf[slot, here, :]
            ds = (w.astype(F32) * (dp - mean)).astype(BF)
            acc = acc + mm(kt[:, here], ds)
            dkv[here, :] += mm(ds, cq) + mm(w, cg)
        acc = acc * (factor * scale)
        two = jnp.concatenate([acc[:, :ROWS], acc[:, ROWS:]], axis=0)
        dq_send[i] = two.T.astype(BF)

        def send(d, _):
            dq_copy(i, (z + d) % NZ).start()
            return 0

        lax.fori_loop(1, NZ, send, 0)

    def turn(i, _):
        @pl.when(i < SLOTS)
        def _():
            scores_phase(i)

        @pl.when(i > 0)
        def _():
            grads_phase(i - 1)

        return 0

    lax.fori_loop(0, SLOTS + 1, turn, 0)

    mate_rows = pl.ds(pl.multiple_of(KEYS * (1 - core), KEYS), KEYS)
    own_rows = pl.ds(pl.multiple_of(KEYS * core, KEYS), KEYS)
    dkv_send[...] = dkv[mate_rows, :].astype(BF)
    dkv_copy = pltpu.make_async_remote_copy(
        src_ref=dkv_send, dst_ref=dkv_recv,
        send_sem=x_ssem.at[0], recv_sem=x_rsem.at[0],
        device_id=mate, device_id_type=MESH,
    )
    dkv_copy.start()

    def reduce(i, _):
        def arrive(d, _):
            dq_arrival(i, (z + d) % NZ).wait_recv()
            return 0

        lax.fori_loop(1, NZ, arrive, 0)
        piece = dq_send[i, pl.ds(pl.multiple_of(PIECE * z, PIECE), PIECE), :].astype(F32)

        def add(d, piece):
            return piece + dq_recv[i, (z + d) % NZ].astype(F32)

        piece = lax.fori_loop(1, NZ, add, piece)
        for c in range(2):
            dq_red[c, par, block_of(i)] = piece[c * SMALL : (c + 1) * SMALL, :]
        return 0

    lax.fori_loop(0, SLOTS, reduce, 0)
    dq_mate = pltpu.make_async_remote_copy(
        src_ref=dq_red.at[1 - core, par], dst_ref=dq_red.at[1 - core, par],
        send_sem=x_ssem.at[1], recv_sem=x_rsem.at[1],
        device_id=mate, device_id_type=MESH,
    )
    dq_mate.start()
    dq_mate_arrival = pltpu.make_async_remote_copy(
        src_ref=dq_red.at[core, 1 - par], dst_ref=dq_red.at[core, 1 - par],
        send_sem=x_ssem.at[1], recv_sem=x_rsem.at[1],
        device_id=mate, device_id_type=MESH,
    )

    dkv_copy.wait_recv()
    whole = dkv[own_rows, :] + dkv_recv[...].astype(F32)
    dkv_fin[...] = jnp.where(row < length, whole, 0.0).astype(BF)

    def kv_out(to, frm):
        return pltpu.make_async_remote_copy(
            src_ref=dkv_fin.at[pl.ds(pl.multiple_of(OUT_KEYS * to, OUT_KEYS), OUT_KEYS), :],
            dst_ref=kv_tiles.at[frm],
            send_sem=fin_ssem.at[0, to], recv_sem=fin_rsem.at[0, frm],
            device_id=(v, to), device_id_type=MESH,
        )

    def dq_out_copy(to, frm):
        return pltpu.make_async_remote_copy(
            src_ref=dq_red.at[core, to % 2, to // 4],
            dst_ref=dq_tiles.at[frm],
            send_sem=fin_ssem.at[1, to], recv_sem=fin_rsem.at[1, frm],
            device_id=(v, to), device_id_type=MESH,
        )

    def send_kv(d, _):
        kv_out((t + d) % NT, t).start()
        return 0

    def send_dq(d, _):
        dq_out_copy((t + d) % NT, t).start()
        return 0

    lax.fori_loop(1, NT, send_kv, 0)
    kv_tiles[t] = dkv_fin[pl.ds(pl.multiple_of(OUT_KEYS * t, OUT_KEYS), OUT_KEYS), :]
    dq_mate_arrival.wait_recv()
    lax.fori_loop(1, NT, send_dq, 0)
    dq_tiles[t] = dq_red[core, t % 2, t // 4]

    def wait_kv(d, _):
        kv_out((t + d) % NT, (t + d) % NT).wait_recv()
        return 0

    def wait_dq(d, _):
        dq_out_copy((t + d) % NT, (t + d) % NT).wait_recv()
        return 0

    lax.fori_loop(1, NT, wait_kv, 0)
    for p in range(NT // 2):
        cols = slice(p * PAIR, (p + 1) * PAIR)
        a = kv_tiles[2 * p].astype(F32)
        b = kv_tiles[2 * p + 1].astype(F32)
        dk_out[:, cols] = jnp.where(left, a, pltpu.roll(b, HEAD, 1)).astype(BF)
        dv_out[:, cols] = jnp.where(left, pltpu.roll(a, HEAD, 1), b).astype(BF)
    lax.fori_loop(1, NT, wait_dq, 0)
    first = (t // 2) % 2 == 0
    for p in range(NT // 2):
        cols = slice(p * PAIR, (p + 1) * PAIR)
        a = dq_tiles[2 * p]
        b = dq_tiles[2 * p + 1]
        a = jnp.where(first, a, pltpu.roll(a, HEAD, 1))
        b = jnp.where(first, pltpu.roll(b, HEAD, 1), b)
        dq_out[:, cols] = jnp.where(left, a, b).astype(BF)

    kv_copy.wait_send()
    len_copy.wait_send()
    dkv_copy.wait_send()
    dq_mate.wait_send()

    def drain_qg(pair, _):
        @pl.when(2 * pair + par != t)
        def _():
            qg_copy(0, pair).wait_send()
            qg_copy(1, pair).wait_send()

        return 0

    def drain_z(d, _):
        to = (z + d) % NZ
        for i in range(SLOTS):
            stat_copy(i, to).wait_send()
            dq_copy(i, to).wait_send()
        return 0

    def drain_fin(d, _):
        to = (t + d) % NT
        kv_out(to, t).wait_send()
        dq_out_copy(to, t).wait_send()
        return 0

    lax.fori_loop(0, NT // 2, drain_qg, 0)
    lax.fori_loop(1, NZ, drain_z, 0)
    lax.fori_loop(1, NT, drain_fin, 0)


def local(queries, keys, values, grad_out, lengths):
    dma = pltpu.SemaphoreType.DMA
    vm = pltpu.VMEM
    return pl.pallas_call(
        kernel,
        out_shape=(
            jax.ShapeDtypeStruct((SMALL, NT * HEAD), BF),
            jax.ShapeDtypeStruct((OUT_KEYS, NT * HEAD), BF),
            jax.ShapeDtypeStruct((OUT_KEYS, NT * HEAD), BF),
        ),
        in_specs=[pl.BlockSpec(memory_space=pltpu.SMEM)]
        + [pl.BlockSpec(memory_space=pl.ANY)] * 4,
        out_specs=(pl.BlockSpec(memory_space=pltpu.VMEM),) * 3,
        scratch_shapes=[
            vm((ROWS, NT * HEAD), BF), vm((ROWS, NT * HEAD), BF),
            vm((KEYS, PAIR), BF), vm((KEYS, PAIR), BF),
            vm((NT * HEAD, ROWS), BF), vm((NT * HEAD, ROWS), BF),
            vm((SLOTS, PAIR, BLOCK), BF),
            vm((2, KEYS, PAIR), BF), vm((2, 8, PAIR), F32),
            vm((BOTH, PAIR), BF), vm((BOTH, PAIR), BF),
            vm((HEAD, BOTH), BF), vm((PAIR, BOTH), BF),
            vm((BOTH, BLOCK), F32), vm((2, BOTH, BLOCK), BF),
            vm((BOTH, PAIR), F32), vm((SLOTS, NZ, 8, ROWS), F32),
            vm((SLOTS, ROWS, PAIR), BF), vm((SLOTS, NZ, PIECE, PAIR), BF),
            vm((2, 2, SLOTS, SMALL, PAIR), F32),
            vm((KEYS, PAIR), BF), vm((KEYS, PAIR), BF), vm((KEYS, PAIR), BF),
            vm((NT, OUT_KEYS, PAIR), BF), vm((NT, SMALL, PAIR), F32),
            dma((4,)), dma((2, NT // 2)), dma((2, NT // 2)), dma((2,)), dma((2,)),
            dma((SLOTS, NZ)), dma((SLOTS, NZ)), dma((SLOTS, NZ)), dma((SLOTS, NZ)),
            dma((2,)), dma((2,)), dma((2, NT)), dma((2, NT)),
        ],
        compiler_params=pltpu.CompilerParams(
            collective_id=0, has_side_effects=True, vmem_limit_bytes=56 * 2**20
        ),
    )(lengths, queries, grad_out, keys, values)


def solution(mesh):
    in_specs = (P("tok", None), P("view", None), P("view", None), P("tok", None), P("view"))
    out_specs = (P(("tok", "view"), None), P(("view", "tok"), None), P(("view", "tok"), None))
    return jax.shard_map(local, mesh=mesh, in_specs=in_specs, out_specs=out_specs, check_vma=False)
```

```python
import functools

import jax
import jax.numpy as jnp
from jax import lax
from jax.experimental import pallas as pl
from jax.experimental.pallas import tpu as pltpu
from jax.sharding import PartitionSpec as P

HEAD = 64
PAIR = 128
ROWS = 384
BLOCK = 2 * ROWS
KEYS = 1024
BOTH = 2 * KEYS
NZ = 8
NT = 16
SLOTS = 4
PIECE = ROWS // NZ
SMALL = PIECE // 2
OUT_KEYS = KEYS // NT
STEP1 = 256
STEP2 = 512
HALF = 512
PAD = 32
MESH = pl.DeviceIdType.MESH
BF = jnp.bfloat16
F32 = jnp.float32
NN = (((1,), (0,)), ((), ()))


def mm(a, b):
    return lax.dot_general(a, b, NN, preferred_element_type=F32)


def kernel(
    len_ref, q_hbm, g_hbm, k_hbm, v_hbm,
    kv_tiles, dq_tiles,
    q_v, g_v, k_v, v_v, turned, qgt, qg_buf, kv_buf, len_buf,
    k0, v0, kt, vt1, s_ref, w_buf, ds_buf, dkv, stats, tops,
    dq_send, dq_recv, dq_fin, dkv_send, dkv_recv, dkv_fin,
    load_sem, qg_ssem, qg_rsem, kv_ssem, kv_rsem, st_ssem, st_rsem,
    dq_ssem, dq_rsem, x_ssem, x_rsem, kvf_ssem, kvf_rsem, dqf_ssem, dqf_rsem, self_sem,
):
    v = lax.axis_index("view")
    t = lax.axis_index("tok")
    z = v // 2
    core = v % 2
    y = t // 4
    par = (t + core) % 2
    other = 2 * z + 1 - core
    scale = HEAD ** -0.5

    pair_cols = pl.ds(pl.multiple_of(PAIR * (t // 2), PAIR), PAIR)
    loads = [
        pltpu.make_async_copy(k_hbm.at[:, pair_cols], k_v, load_sem.at[0]),
        pltpu.make_async_copy(v_hbm.at[:, pair_cols], v_v, load_sem.at[1]),
        pltpu.make_async_copy(q_hbm, q_v, load_sem.at[2]),
        pltpu.make_async_copy(g_hbm, g_v, load_sem.at[3]),
    ]
    for load in loads:
        load.start()

    barrier = pltpu.get_barrier_semaphore()

    def greet(view, tok):
        pl.semaphore_signal(barrier, inc=1, device_id=(view, tok), device_id_type=MESH)

    def greet_tok(d, _):
        greet(v, (t + d) % NT)
        return 0

    def greet_z(d, _):
        greet(2 * ((z + d) % NZ) + core, t)
        return 0

    def greet_other(d, _):
        tok = 2 * d + 1 - par

        @pl.when(tok != t)
        def _():
            greet(other, tok)

        return 0

    greet(other, t)
    lax.fori_loop(1, NT, greet_tok, 0)
    lax.fori_loop(0, NT // 2, greet_other, 0)
    lax.fori_loop(1, NZ, greet_z, 0)

    length = len_ref[0]
    lane = lax.broadcasted_iota(jnp.int32, (1, PAIR), 1)
    left = lane < HEAD
    row = lax.broadcasted_iota(jnp.int32, (KEYS, 1), 0)
    loads[0].wait()
    loads[1].wait()
    even = t % 2 == 0
    k_f = k_v[...].astype(F32)
    v_f = v_v[...].astype(F32)
    k_left = jnp.where(even, k_f, pltpu.roll(k_f, HEAD, 1))
    v_right = jnp.where(even, pltpu.roll(v_f, HEAD, 1), v_f)
    kv = jnp.where(left, k_left, v_right)
    kv = jnp.where(row < length, kv, kv[0:1, :])
    kv_buf[core] = kv.astype(BF)
    len_buf[core] = jnp.full((8, PAIR), length, jnp.int32).astype(F32)

    loads[2].wait()
    loads[3].wait()
    chosen = pl.ds(pl.multiple_of(HEAD * par, HEAD), HEAD)

    def pack(pair, _):
        cols = pl.ds(pl.multiple_of(PAIR * pair, PAIR), PAIR)
        turned[0] = q_v[:, cols].T
        turned[1] = g_v[:, cols].T
        qgt[pair, 0:HEAD, :] = turned[0, chosen, :]
        qgt[pair, HEAD:PAIR, :] = turned[1, chosen, :]
        return 0

    lax.fori_loop(0, NT // 2, pack, 0)

    col = lax.broadcasted_iota(jnp.int32, (1, KEYS), 1).astype(F32)
    sub = lax.broadcasted_iota(jnp.int32, (HEAD, 1), 0)

    def prepare(side):
        here = pl.ds(pl.multiple_of(KEYS * side, KEYS), KEYS)
        tile = kv_buf[side]
        f = tile.astype(F32)
        k0[here, :] = jnp.where(left, f, 0.0).astype(BF)
        v0[here, :] = jnp.where(left, 0.0, f).astype(BF)
        flipped = tile.T.astype(F32)
        okay = jnp.where(col < len_buf[side][0:1, 0:1], 1.0, 0.0)
        kt[:, here] = (flipped[0:HEAD] * okay).astype(BF)
        vt1[HEAD:PAIR, here] = (flipped[HEAD:PAIR] * okay).astype(BF)
        vt1[0:HEAD, here] = jnp.where(sub == 0, okay, 0.0).astype(BF)

    prepare(core)
    dkv[...] = jnp.zeros_like(dkv)

    pl.semaphore_wait(barrier, 1 + NT - 1 + NT // 2 - (1 - core) + NZ - 1)

    kv_copy = pltpu.make_async_remote_copy(
        src_ref=kv_buf.at[core], dst_ref=kv_buf.at[core],
        send_sem=kv_ssem.at[0], recv_sem=kv_rsem.at[0],
        device_id=(other, t), device_id_type=MESH,
    )
    len_copy = pltpu.make_async_remote_copy(
        src_ref=len_buf.at[core], dst_ref=len_buf.at[core],
        send_sem=kv_ssem.at[1], recv_sem=kv_rsem.at[1],
        device_id=(other, t), device_id_type=MESH,
    )
    kv_copy.start()
    len_copy.start()

    def qg_copy(pair):
        return pltpu.make_async_remote_copy(
            src_ref=qgt.at[pair], dst_ref=qg_buf.at[y, (t // 2) % 2],
            send_sem=qg_ssem.at[pair], recv_sem=qg_rsem.at[t // 2],
            device_id=(v, 2 * pair + par), device_id_type=MESH,
        )

    def send_row(j):
        for half in range(2):
            pair = 2 * ((y + j) % 4) + half

            @pl.when(2 * pair + par != t)
            def _():
                qg_copy(pair).start()

            @pl.when(2 * pair + par == t)
            def _():
                qg_buf[y, half] = qgt[pair]

    send_row(0)
    send_row(1)

    kv_copy.wait_recv()
    len_copy.wait_recv()
    prepare(1 - core)

    def stat_copy(i, to, frm):
        return pltpu.make_async_remote_copy(
            src_ref=stats.at[i, frm], dst_ref=stats.at[i, frm],
            send_sem=st_ssem.at[i, to], recv_sem=st_rsem.at[i, frm],
            device_id=(2 * to + core, t), device_id_type=MESH,
        )

    def dq_copy(i, to, frm):
        return pltpu.make_async_remote_copy(
            src_ref=dq_send.at[i, pl.ds(pl.multiple_of(PIECE * to, PIECE), PIECE), :],
            dst_ref=dq_recv.at[i, frm],
            send_sem=dq_ssem.at[i, to], recv_sem=dq_rsem.at[i, frm],
            device_id=(2 * to + core, t), device_id_type=MESH,
        )

    def block_of(i):
        return (y + 3 * i) % 4

    def queries_of(i):
        sb = block_of(i)
        return jnp.concatenate([qg_buf[sb, 0], qg_buf[sb, 1]], axis=1)

    def scores_phase(i):
        sb = block_of(i)
        slot = i % 2
        for half in range(2):
            source = 4 * sb + 2 * half + par

            @pl.when(source != t)
            def _():
                pltpu.make_async_remote_copy(
                    src_ref=qgt.at[0], dst_ref=qg_buf.at[sb, half],
                    send_sem=qg_ssem.at[0], recv_sem=qg_rsem.at[2 * sb + half],
                    device_id=(v, source), device_id_type=MESH,
                ).wait_recv()

        @pl.when(i < 2)
        def _():
            send_row(i + 2)

        qg = queries_of(i)
        top = jnp.full((8, BLOCK), -3e38, F32)
        for k in range(BOTH // STEP1):
            here = slice(k * STEP1, (k + 1) * STEP1)
            s = mm(k0[here, :], qg)
            s_ref[here, :] = s
            top = jnp.maximum(top, jnp.max(s.reshape(STEP1 // 8, 8, BLOCK), axis=0))
        top = jnp.max(top, axis=0, keepdims=True)
        acc = jnp.zeros((PAIR, BLOCK), F32)
        for k in range(BOTH // STEP1):
            here = slice(k * STEP1, (k + 1) * STEP1)
            w = jnp.exp((s_ref[here, :] - top) * scale).astype(BF)
            w_buf[slot, here, :] = w
            acc = acc + mm(vt1[:, here], w)
        total = acc[0:1, :]
        mean = jnp.sum(acc[HEAD:, :] * qg[HEAD:, :].astype(F32), axis=0, keepdims=True)
        top = top * scale
        tops[slot] = top
        stats[i, z, 0:1, :] = top + jnp.log(total)
        stats[i, z, 1:2, :] = mean / total

        def send(d, _):
            stat_copy(i, (z + d) % NZ, z).start()
            return 0

        lax.fori_loop(1, NZ, send, 0)

    def combine(i):
        def arrive(d, _):
            frm = (z + d) % NZ
            stat_copy(i, frm, frm).wait_recv()
            return 0

        lax.fori_loop(1, NZ, arrive, 0)
        logs = stats[i, :, 0, :]
        peak = jnp.max(logs, axis=0, keepdims=True)
        weight = jnp.exp(logs - peak)
        total = jnp.sum(weight, axis=0, keepdims=True)
        mean = jnp.sum(stats[i, :, 1, :] * weight, axis=0, keepdims=True) / total
        factor = jnp.exp(tops[i % 2] - peak) / total
        qg = queries_of(i)
        scaled = (qg.astype(F32) * factor).T
        cq = jnp.where(left, scaled * scale, 0.0).astype(BF)
        cg = jnp.where(left, 0.0, scaled).astype(BF)
        return qg, mean, factor, cq, cg

    def give_dq(i, acc, factor):
        acc = acc * (factor * scale)
        two = jnp.concatenate([acc[:, :ROWS], acc[:, ROWS:]], axis=0)
        dq_send[i] = two.T.astype(BF)

        def send(d, _):
            dq_copy(i, (z + d) % NZ, z).start()
            return 0

        lax.fori_loop(1, NZ, send, 0)

    def grads_phase(i):
        slot = i % 2
        qg, mean, factor, cq, cg = combine(i)
        acc = jnp.zeros((HEAD, BLOCK), F32)
        for k in range(BOTH // STEP2):
            here = slice(k * STEP2, (k + 1) * STEP2)
            dp = mm(v0[here, :], qg)
            w = w_buf[slot, here, :]
            ds = (w.astype(F32) * (dp - mean)).astype(BF)
            acc = acc + mm(kt[:, here], ds)
            dkv[here, :] += mm(ds, cq) + mm(w, cg)
        give_dq(i, acc, factor)

    def dq_give(i, half, c):
        return pltpu.make_async_remote_copy(
            src_ref=dq_fin.at[i, c], dst_ref=dq_tiles.at[t],
            send_sem=dqf_ssem.at[i, half, c], recv_sem=dqf_rsem.at[t],
            device_id=(2 * z + c, 4 * block_of(i) + 2 * half + par), device_id_type=MESH,
        )

    def own_piece(i, half, c):
        return jnp.logical_and(4 * block_of(i) + 2 * half + par == t, c == core)

    def reduce(i):
        def arrive(d, _):
            frm = (z + d) % NZ
            dq_copy(i, frm, frm).wait_recv()
            return 0

        lax.fori_loop(1, NZ, arrive, 0)
        piece = dq_send[i, pl.ds(pl.multiple_of(PIECE * z, PIECE), PIECE), :].astype(F32)

        def add(d, piece):
            return piece + dq_recv[i, (z + d) % NZ].astype(F32)

        piece = lax.fori_loop(1, NZ, add, piece)
        fill = jnp.zeros((PAD - SMALL, PAIR), F32)
        for c in range(2):
            rows = piece[c * SMALL : (c + 1) * SMALL, :]
            dq_fin[i, c] = jnp.concatenate([rows, fill], axis=0).astype(BF)
        for half in range(2):
            for c in range(2):
                @pl.when(jnp.logical_not(own_piece(i, half, c)))
                def _():
                    dq_give(i, half, c).start()

                @pl.when(own_piece(i, half, c))
                def _():
                    keep = pltpu.make_async_copy(dq_fin.at[i, c], dq_tiles.at[t], self_sem.at[0])
                    keep.start()
                    keep.wait()

    def turn(i, _):
        scores_phase(i)

        @pl.when(i > 0)
        def _():
            grads_phase(i - 1)

        @pl.when(i > 1)
        def _():
            reduce(i - 2)

        return 0

    lax.fori_loop(0, SLOTS, turn, 0)

    last = SLOTS - 1
    qg, mean, factor, cq, cg = combine(last)
    acc = jnp.zeros((HEAD, BLOCK), F32)
    for k in range(BOTH // STEP2):
        here = slice(k * STEP2, (k + 1) * STEP2)
        dp = mm(v0[here, :], qg)
        ds = (w_buf[last % 2, here, :].astype(F32) * (dp - mean)).astype(BF)
        ds_buf[here, :] = ds
        acc = acc + mm(kt[:, here], ds)
    give_dq(last, acc, factor)

    def dkv_copy(j):
        return pltpu.make_async_remote_copy(
            src_ref=dkv_send.at[j], dst_ref=dkv_recv.at[j],
            send_sem=x_ssem.at[j], recv_sem=x_rsem.at[j],
            device_id=(other, t), device_id_type=MESH,
        )

    def kv_out(to, frm):
        return pltpu.make_async_remote_copy(
            src_ref=dkv_fin.at[pl.ds(pl.multiple_of(OUT_KEYS * to, OUT_KEYS), OUT_KEYS), :],
            dst_ref=kv_tiles.at[frm],
            send_sem=kvf_ssem.at[to], recv_sem=kvf_rsem.at[frm],
            device_id=(v, to), device_id_type=MESH,
        )

    def kv_total(side, j):
        here = pl.ds(pl.multiple_of(KEYS * side + HALF * j, HALF), HALF)
        return dkv[here, :] + mm(ds_buf[here, :], cq) + mm(w_buf[last % 2, here, :], cg)

    for j in range(2):
        dkv_send[j] = kv_total(1 - core, j).astype(BF)
        dkv_copy(j).start()
    reduce(last - 1)
    kv_self = pltpu.make_async_copy(
        dkv_fin.at[pl.ds(pl.multiple_of(OUT_KEYS * t, OUT_KEYS), OUT_KEYS), :],
        kv_tiles.at[t], self_sem.at[1],
    )
    for j in range(2):
        whole = kv_total(core, j)
        dkv_copy(j).wait_recv()
        whole = whole + dkv_recv[j].astype(F32)
        rows = slice(j * HALF, (j + 1) * HALF)
        dkv_fin[rows, :] = jnp.where(row[rows] < length, whole, 0.0).astype(BF)

        def send(d, _):
            to = NT // 2 * j + (t + d) % (NT // 2)

            @pl.when(to != t)
            def _():
                kv_out(to, t).start()

            @pl.when(to == t)
            def _():
                kv_self.start()

            return 0

        lax.fori_loop(0, NT // 2, send, 0)
    reduce(last)

    kv_copy.wait_send()
    len_copy.wait_send()
    dkv_copy(0).wait_send()
    dkv_copy(1).wait_send()
    kv_self.wait()

    def drain_qg(pair, _):
        @pl.when(2 * pair + par != t)
        def _():
            qg_copy(pair).wait_send()

        return 0

    def drain_z(d, _):
        to = (z + d) % NZ
        for i in range(SLOTS):
            stat_copy(i, to, z).wait_send()
            dq_copy(i, to, z).wait_send()
        return 0

    def drain_dq(i, _):
        for half in range(2):
            for c in range(2):
                @pl.when(jnp.logical_not(own_piece(i, half, c)))
                def _():
                    dq_give(i, half, c).wait_send()

        return 0

    def drain_kv(d, _):
        kv_out((t + d) % NT, t).wait_send()
        return 0

    def arrive_kv(d, _):
        frm = (t + d) % NT
        kv_out(frm, frm).wait_recv()
        return 0

    def arrive_dq(frm, _):
        @pl.when(jnp.logical_or(frm != t, core == 1))
        def _():
            pltpu.make_async_remote_copy(
                src_ref=dq_fin.at[0, 0], dst_ref=dq_tiles.at[frm],
                send_sem=dqf_ssem.at[0, 0, 0], recv_sem=dqf_rsem.at[frm],
                device_id=(other, t), device_id_type=MESH,
            ).wait_recv()

        return 0

    lax.fori_loop(0, NT // 2, drain_qg, 0)
    lax.fori_loop(1, NZ, drain_z, 0)
    lax.fori_loop(0, SLOTS, drain_dq, 0)
    lax.fori_loop(1, NT, drain_kv, 0)
    lax.fori_loop(1, NT, arrive_kv, 0)
    lax.fori_loop(0, NT, arrive_dq, 0)


def assemble(kv_tiles, dq_tiles, dq_out, dk_out, dv_out):
    t = lax.axis_index("tok")
    left = lax.broadcasted_iota(jnp.int32, (1, PAIR), 1) < HEAD
    first = (t // 2) % 2 == 0
    for p in range(NT // 2):
        cols = slice(p * PAIR, (p + 1) * PAIR)
        a = kv_tiles[2 * p].astype(F32)
        b = kv_tiles[2 * p + 1].astype(F32)
        dk_out[:, cols] = jnp.where(left, a, pltpu.roll(b, HEAD, 1)).astype(BF)
        dv_out[:, cols] = jnp.where(left, pltpu.roll(a, HEAD, 1), b).astype(BF)
        a = dq_tiles[2 * p].astype(F32)[0:SMALL]
        b = dq_tiles[2 * p + 1].astype(F32)[0:SMALL]
        a = jnp.where(first, a, pltpu.roll(a, HEAD, 1))
        b = jnp.where(first, pltpu.roll(b, HEAD, 1), b)
        dq_out[:, cols] = jnp.where(left, a, b).astype(BF)


def local(queries, keys, values, grad_out, lengths):
    dma = pltpu.SemaphoreType.DMA
    vm = pltpu.VMEM
    kv_tiles, dq_tiles = pl.pallas_call(
        kernel,
        out_shape=(
            jax.ShapeDtypeStruct((NT, OUT_KEYS, PAIR), BF),
            jax.ShapeDtypeStruct((NT, PAD, PAIR), BF),
        ),
        in_specs=[pl.BlockSpec(memory_space=pltpu.SMEM)]
        + [pl.BlockSpec(memory_space=pl.ANY)] * 4,
        out_specs=(pl.BlockSpec(memory_space=pl.ANY),) * 2,
        scratch_shapes=[
            vm((ROWS, NT * HEAD), BF), vm((ROWS, NT * HEAD), BF),
            vm((KEYS, PAIR), BF), vm((KEYS, PAIR), BF),
            vm((2, PAIR, ROWS), BF), vm((NT // 2, PAIR, ROWS), BF),
            vm((SLOTS, 2, PAIR, ROWS), BF),
            vm((2, KEYS, PAIR), BF), vm((2, 8, PAIR), F32),
            vm((BOTH, PAIR), BF), vm((BOTH, PAIR), BF),
            vm((HEAD, BOTH), BF), vm((PAIR, BOTH), BF),
            vm((BOTH, BLOCK), F32), vm((2, BOTH, BLOCK), BF), vm((BOTH, BLOCK), BF),
            vm((BOTH, PAIR), F32), vm((SLOTS, NZ, 2, BLOCK), F32), vm((2, 1, BLOCK), F32),
            vm((SLOTS, ROWS, PAIR), BF), vm((SLOTS, NZ, PIECE, PAIR), BF),
            vm((SLOTS, 2, PAD, PAIR), BF),
            vm((2, HALF, PAIR), BF), vm((2, HALF, PAIR), BF), vm((KEYS, PAIR), BF),
            dma((4,)), dma((NT // 2,)), dma((NT // 2,)), dma((2,)), dma((2,)),
            dma((SLOTS, NZ)), dma((SLOTS, NZ)), dma((SLOTS, NZ)), dma((SLOTS, NZ)),
            dma((2,)), dma((2,)), dma((NT,)), dma((NT,)),
            dma((SLOTS, 2, 2)), dma((NT,)), dma((2,)),
        ],
        compiler_params=pltpu.CompilerParams(
            collective_id=0, has_side_effects=True, vmem_limit_bytes=56 * 2**20
        ),
    )(lengths, queries, grad_out, keys, values)
    return pl.pallas_call(
        assemble,
        out_shape=(
            jax.ShapeDtypeStruct((SMALL, NT * HEAD), BF),
            jax.ShapeDtypeStruct((OUT_KEYS, NT * HEAD), BF),
            jax.ShapeDtypeStruct((OUT_KEYS, NT * HEAD), BF),
        ),
        in_specs=[pl.BlockSpec(memory_space=pltpu.VMEM)] * 2,
        out_specs=(pl.BlockSpec(memory_space=pltpu.VMEM),) * 3,
    )(kv_tiles, dq_tiles)


def solution(mesh):
    in_specs = (P("tok", None), P("view", None), P("view", None), P("tok", None), P("view"))
    out_specs = (P(("tok", "view"), None), P(("view", "tok"), None), P(("view", "tok"), None))
    return jax.shard_map(local, mesh=mesh, in_specs=in_specs, out_specs=out_specs, check_vma=False)
```

```python
import functools

import jax
import jax.numpy as jnp
from jax import lax
from jax.experimental import pallas as pl
from jax.experimental.pallas import tpu as pltpu
from jax.sharding import PartitionSpec as P

HEAD = 64
PAIR = 128
ROWS = 384
BLOCK = 2 * ROWS
KEYS = 1024
BOTH = 2 * KEYS
NZ = 8
NT = 16
SLOTS = 4
PIECE = ROWS // NZ
SMALL = PIECE // 2
OUT_KEYS = KEYS // NT
STEP1 = 512
LOG2E = 1.4426950408889634
STEP2 = 1024
HALF = 512
ROW = KEYS // 4
PAD = 32
MESH = pl.DeviceIdType.MESH
BF = jnp.bfloat16
F32 = jnp.float32
NN = (((1,), (0,)), ((), ()))


def mm(a, b):
    return lax.dot_general(a, b, NN, preferred_element_type=F32)


def kernel(
    len_ref, q_hbm, g_hbm, k_hbm, v_hbm,
    kv_tiles, dq_tiles,
    q_v, g_v, k_v, v_v, turned, qgt, qg_buf, kv_buf, len_buf,
    k0, v0, kt, vt1, s_ref, w_buf, ds_buf, cq_buf, cg_buf, stats, tops,
    dq_send, dq_recv, dq_fin, dkv, dkv_send, dkv_recv, dkv_fin,
    load_sem, qg_ssem, qg_rsem, kv_ssem, kv_rsem, st_ssem, st_rsem,
    dq_ssem, dq_rsem, x_ssem, x_rsem, kvf_ssem, kvf_rsem, dqf_ssem, dqf_rsem, self_sem,
):
    v = lax.axis_index("view")
    t = lax.axis_index("tok")
    z = v // 2
    core = v % 2
    y = t // 4
    par = (t + core) % 2
    other = 2 * z + 1 - core
    scale = HEAD ** -0.5

    pair_cols = pl.ds(pl.multiple_of(PAIR * (t // 2), PAIR), PAIR)
    loads = [
        pltpu.make_async_copy(q_hbm, q_v, load_sem.at[0]),
        pltpu.make_async_copy(g_hbm, g_v, load_sem.at[1]),
        pltpu.make_async_copy(k_hbm.at[:, pair_cols], k_v, load_sem.at[2]),
        pltpu.make_async_copy(v_hbm.at[:, pair_cols], v_v, load_sem.at[3]),
    ]
    for load in loads:
        load.start()

    barrier = pltpu.get_barrier_semaphore()

    def greet(view, tok):
        pl.semaphore_signal(barrier, inc=1, device_id=(view, tok), device_id_type=MESH)

    def greet_tok(d, _):
        greet(v, (t + d) % NT)
        return 0

    def greet_z(d, _):
        greet(2 * ((z + d) % NZ) + core, t)
        return 0

    def greet_other(d, _):
        tok = 2 * d + 1 - par

        @pl.when(tok != t)
        def _():
            greet(other, tok)

        return 0

    greet(other, t)
    lax.fori_loop(1, NT, greet_tok, 0)
    lax.fori_loop(0, NT // 2, greet_other, 0)
    lax.fori_loop(1, NZ, greet_z, 0)

    loads[0].wait()
    loads[1].wait()
    chosen = pl.ds(pl.multiple_of(HEAD * par, HEAD), HEAD)

    def pack(j, _):
        pair = (2 * y + j) % (NT // 2)
        cols = pl.ds(pl.multiple_of(PAIR * pair, PAIR), PAIR)
        turned[0] = q_v[:, cols].T
        turned[1] = g_v[:, cols].T
        qgt[pair, 0:HEAD, :] = turned[0, chosen, :]
        qgt[pair, HEAD:PAIR, :] = turned[1, chosen, :]
        return 0


    lax.fori_loop(0, 2, pack, 0)
    pl.semaphore_wait(barrier, 1 + NT - 1 + NT // 2 - (1 - core) + NZ - 1)

    def qg_copy(pair):
        return pltpu.make_async_remote_copy(
            src_ref=qgt.at[pair], dst_ref=qg_buf.at[y, (t // 2) % 2],
            send_sem=qg_ssem.at[pair], recv_sem=qg_rsem.at[t // 2],
            device_id=(v, 2 * pair + par), device_id_type=MESH,
        )

    def send_row(j):
        for half in range(2):
            pair = 2 * ((y + j) % 4) + half

            @pl.when(2 * pair + par != t)
            def _():
                qg_copy(pair).start()

            @pl.when(2 * pair + par == t)
            def _():
                qg_buf[y, half] = qgt[pair]

    send_row(0)
    lax.fori_loop(2, 4, pack, 0)
    send_row(1)

    length = len_ref[0]
    left = lax.broadcasted_iota(jnp.int32, (1, PAIR), 1) < HEAD
    row = lax.broadcasted_iota(jnp.int32, (KEYS, 1), 0)
    loads[2].wait()
    loads[3].wait()
    even = t % 2 == 0
    k_f = k_v[...].astype(F32)
    v_f = v_v[...].astype(F32)
    k_left = jnp.where(even, k_f, pltpu.roll(k_f, HEAD, 1))
    v_right = jnp.where(even, pltpu.roll(v_f, HEAD, 1), v_f)
    kv = jnp.where(left, k_left, v_right)
    kv = jnp.where(row < length, kv, kv[0:1, :])
    kv_buf[core] = kv.astype(BF)
    len_buf[core] = jnp.full((8, PAIR), length, jnp.int32).astype(F32)

    kv_copy = pltpu.make_async_remote_copy(
        src_ref=kv_buf.at[core], dst_ref=kv_buf.at[core],
        send_sem=kv_ssem.at[0], recv_sem=kv_rsem.at[0],
        device_id=(other, t), device_id_type=MESH,
    )
    len_copy = pltpu.make_async_remote_copy(
        src_ref=len_buf.at[core], dst_ref=len_buf.at[core],
        send_sem=kv_ssem.at[1], recv_sem=kv_rsem.at[1],
        device_id=(other, t), device_id_type=MESH,
    )
    kv_copy.start()
    len_copy.start()

    lax.fori_loop(4, NT // 2, pack, 0)

    col = lax.broadcasted_iota(jnp.int32, (1, KEYS), 1).astype(F32)
    sub = lax.broadcasted_iota(jnp.int32, (HEAD, 1), 0)

    def prepare(side):
        here = pl.ds(pl.multiple_of(KEYS * side, KEYS), KEYS)
        tile = kv_buf[side]
        f = tile.astype(F32)
        k0[here, :] = jnp.where(left, f, 0.0).astype(BF)
        v0[here, :] = jnp.where(left, 0.0, f).astype(BF)
        flipped = tile.T.astype(F32)
        okay = jnp.where(col < len_buf[side][0:1, 0:1], 1.0, 0.0)
        kt[:, here] = (flipped[0:HEAD] * okay).astype(BF)
        vt1[HEAD:PAIR, here] = (flipped[HEAD:PAIR] * okay).astype(BF)
        vt1[0:HEAD, here] = jnp.where(sub == 0, okay, 0.0).astype(BF)


    prepare(core)
    kv_copy.wait_recv()
    len_copy.wait_recv()
    prepare(1 - core)

    def stat_copy(i, to, frm):
        return pltpu.make_async_remote_copy(
            src_ref=stats.at[i, frm], dst_ref=stats.at[i, frm],
            send_sem=st_ssem.at[i, to], recv_sem=st_rsem.at[i, frm],
            device_id=(2 * to + core, t), device_id_type=MESH,
        )

    def dq_copy(i, to, frm):
        return pltpu.make_async_remote_copy(
            src_ref=dq_send.at[i, pl.ds(pl.multiple_of(PIECE * to, PIECE), PIECE), :],
            dst_ref=dq_recv.at[i, frm],
            send_sem=dq_ssem.at[i, to], recv_sem=dq_rsem.at[i, frm],
            device_id=(2 * to + core, t), device_id_type=MESH,
        )

    def far(d):
        return NZ // 2 + (d // 2) * (2 * ((d + 1) % 2) - 1)

    def block_of(i):
        return (y + 3 * i) % 4

    def queries_of(i):
        sb = block_of(i)
        return jnp.concatenate([qg_buf[sb, 0], qg_buf[sb, 1]], axis=1)

    def scores_phase(i):
        sb = block_of(i)
        for half in range(2):
            source = 4 * sb + 2 * half + par

            @pl.when(source != t)
            def _():
                pltpu.make_async_remote_copy(
                    src_ref=qgt.at[0], dst_ref=qg_buf.at[sb, half],
                    send_sem=qg_ssem.at[0], recv_sem=qg_rsem.at[2 * sb + half],
                    device_id=(v, source), device_id_type=MESH,
                ).wait_recv()

        @pl.when(i < 2)
        def _():
            send_row(i + 2)

        qg = queries_of(i)
        top = jnp.full((8, BLOCK), -3e38, F32)
        for k in range(BOTH // STEP1):
            here = slice(k * STEP1, (k + 1) * STEP1)
            s = mm(k0[here, :], qg)
            s_ref[here, :] = s
            top = jnp.maximum(top, jnp.max(s.reshape(STEP1 // 8, 8, BLOCK), axis=0))
        top = jnp.max(top, axis=0, keepdims=True)
        for k in range(BOTH // STEP1):
            here = slice(k * STEP1, (k + 1) * STEP1)
            w_buf[i, here, :] = jnp.exp2((s_ref[here, :] - top) * (scale * LOG2E)).astype(BF)
        acc = mm(vt1[...], w_buf[i])
        total = acc[0:1, :]
        mean = jnp.sum(acc[HEAD:, :] * qg[HEAD:, :].astype(F32), axis=0, keepdims=True)
        top = top * scale
        tops[i] = top
        stats[i, z, 0:1, :] = top + jnp.log(total)
        stats[i, z, 1:2, :] = mean / total

        def send(d, _):
            stat_copy(i, (z + far(d)) % NZ, z).start()
            return 0

        lax.fori_loop(1, NZ, send, 0)

    def combine(i):
        def arrive(d, _):
            frm = (z + d) % NZ
            stat_copy(i, frm, frm).wait_recv()
            return 0

        lax.fori_loop(1, NZ, arrive, 0)
        logs = stats[i, :, 0, :]
        peak = jnp.max(logs, axis=0, keepdims=True)
        weight = jnp.exp(logs - peak)
        total = jnp.sum(weight, axis=0, keepdims=True)
        mean = jnp.sum(stats[i, :, 1, :] * weight, axis=0, keepdims=True) / total
        factor = jnp.exp(tops[i] - peak) / total
        qg = queries_of(i)
        scaled = (qg.astype(F32) * factor).T
        cq_buf[i] = jnp.where(left, scaled * scale, 0.0).astype(BF)
        cg_buf[i] = jnp.where(left, 0.0, scaled).astype(BF)
        return qg, mean, factor

    def give_dq(i, acc, factor):
        acc = acc * (factor * scale)
        two = jnp.concatenate([acc[:, :ROWS], acc[:, ROWS:]], axis=0)
        dq_send[i] = two.T.astype(BF)

        def send(d, _):
            dq_copy(i, (z + far(d)) % NZ, z).start()
            return 0

        lax.fori_loop(1, NZ, send, 0)

    def grads_phase(i):
        qg, mean, factor = combine(i)
        acc = jnp.zeros((HEAD, BLOCK), F32)
        for k in range(BOTH // STEP2):
            here = slice(k * STEP2, (k + 1) * STEP2)
            dp = mm(v0[here, :], qg)
            ds = (w_buf[i, here, :].astype(F32) * (dp - mean)).astype(BF)
            ds_buf[i, here, :] = ds
            acc = acc + mm(kt[:, here], ds)
        give_dq(i, acc, factor)

    def dq_give(i, half, c):
        return pltpu.make_async_remote_copy(
            src_ref=dq_fin.at[i, c], dst_ref=dq_tiles.at[t],
            send_sem=dqf_ssem.at[i, half, c], recv_sem=dqf_rsem.at[t],
            device_id=(2 * z + c, 4 * block_of(i) + 2 * half + par), device_id_type=MESH,
        )

    def own_piece(i, half, c):
        return jnp.logical_and(4 * block_of(i) + 2 * half + par == t, c == core)

    def reduce(i):
        def arrive(d, _):
            frm = (z + d) % NZ
            dq_copy(i, frm, frm).wait_recv()
            return 0

        lax.fori_loop(1, NZ, arrive, 0)
        piece = dq_send[i, pl.ds(pl.multiple_of(PIECE * z, PIECE), PIECE), :].astype(F32)

        def add(d, piece):
            return piece + dq_recv[i, (z + d) % NZ].astype(F32)

        piece = lax.fori_loop(1, NZ, add, piece)
        fill = jnp.zeros((PAD - SMALL, PAIR), F32)
        for c in range(2):
            rows = piece[c * SMALL : (c + 1) * SMALL, :]
            dq_fin[i, c] = jnp.concatenate([rows, fill], axis=0).astype(BF)
        for half in range(2):
            for c in range(2):
                @pl.when(jnp.logical_not(own_piece(i, half, c)))
                def _():
                    dq_give(i, half, c).start()

                @pl.when(own_piece(i, half, c))
                def _():
                    keep = pltpu.make_async_copy(dq_fin.at[i, c], dq_tiles.at[t], self_sem.at[0])
                    keep.start()
                    keep.wait()

    def kv_sum(here, blocks):
        acc = jnp.zeros((here.size, PAIR), F32)
        for i in blocks:
            acc = acc + mm(ds_buf[i, here, :], cq_buf[i]) + mm(w_buf[i, here, :], cg_buf[i])
        return acc

    def mate_rows(j):
        return pl.ds(pl.multiple_of(KEYS * (1 - core) + HALF * j, HALF), HALF)

    def turn(i, _):
        @pl.when(i < SLOTS)
        def _():
            scores_phase(i)

        @pl.when(i == SLOTS + 1)
        def _():
            for j in range(2):
                dkv[j] = kv_sum(mate_rows(j), (0, 1))

        @pl.when(i > 1)
        def _():
            grads_phase(i - 2)

        @pl.when(i > 3)
        def _():
            reduce(i - 4)

        return 0

    lax.fori_loop(0, SLOTS + 2, turn, 0)

    def dkv_copy(j):
        return pltpu.make_async_remote_copy(
            src_ref=dkv_send.at[j], dst_ref=dkv_recv.at[pl.ds(HALF * j, HALF), :],
            send_sem=x_ssem.at[j], recv_sem=x_rsem.at[j],
            device_id=(other, t), device_id_type=MESH,
        )

    def kv_out(to, frm):
        return pltpu.make_async_remote_copy(
            src_ref=dkv_fin.at[pl.ds(pl.multiple_of(OUT_KEYS * to, OUT_KEYS), OUT_KEYS), :],
            dst_ref=kv_tiles.at[frm],
            send_sem=kvf_ssem.at[to], recv_sem=kvf_rsem.at[frm],
            device_id=(v, to), device_id_type=MESH,
        )

    for j in range(2):
        dkv_send[j] = (dkv[j] + kv_sum(mate_rows(j), (2, 3))).astype(BF)
        dkv_copy(j).start()
    reduce(SLOTS - 2)
    kv_self = pltpu.make_async_copy(
        dkv_fin.at[pl.ds(pl.multiple_of(OUT_KEYS * t, OUT_KEYS), OUT_KEYS), :],
        kv_tiles.at[t], self_sem.at[1],
    )
    row_of = lax.broadcasted_iota(jnp.int32, (ROW, 1), 0)

    def own_rows(j, _):
        to_y = (y + 2 + j * (1 + j) // 2) % 4
        start = pl.multiple_of(ROW * to_y, ROW)
        whole = kv_sum(pl.ds(pl.multiple_of(KEYS * core + start, ROW), ROW), range(SLOTS))

        @pl.when(j == 0)
        def _():
            dkv_copy(0).wait_recv()
            dkv_copy(1).wait_recv()

        rows = pl.ds(start, ROW)
        whole = whole + dkv_recv[rows, :].astype(F32)
        dkv_fin[rows, :] = jnp.where(row_of + start < length, whole, 0.0).astype(BF)

        def send(d, _):
            to = 4 * to_y + (t + 2 + d) % 4

            @pl.when(to != t)
            def _():
                kv_out(to, t).start()

            @pl.when(to == t)
            def _():
                kv_self.start()

            return 0

        lax.fori_loop(0, 4, send, 0)
        return 0

    lax.fori_loop(0, 4, own_rows, 0)
    reduce(SLOTS - 1)

    kv_copy.wait_send()
    len_copy.wait_send()
    dkv_copy(0).wait_send()
    dkv_copy(1).wait_send()
    kv_self.wait()

    def drain_qg(pair, _):
        @pl.when(2 * pair + par != t)
        def _():
            qg_copy(pair).wait_send()

        return 0

    def drain_z(d, _):
        to = (z + d) % NZ
        for i in range(SLOTS):
            stat_copy(i, to, z).wait_send()
            dq_copy(i, to, z).wait_send()
        return 0

    def drain_dq(i, _):
        for half in range(2):
            for c in range(2):
                @pl.when(jnp.logical_not(own_piece(i, half, c)))
                def _():
                    dq_give(i, half, c).wait_send()

        return 0

    def drain_kv(d, _):
        kv_out((t + d) % NT, t).wait_send()
        return 0

    def arrive_kv(d, _):
        frm = (t + d) % NT
        kv_out(frm, frm).wait_recv()
        return 0

    def arrive_dq(frm, _):
        @pl.when(jnp.logical_or(frm != t, core == 1))
        def _():
            pltpu.make_async_remote_copy(
                src_ref=dq_fin.at[0, 0], dst_ref=dq_tiles.at[frm],
                send_sem=dqf_ssem.at[0, 0, 0], recv_sem=dqf_rsem.at[frm],
                device_id=(other, t), device_id_type=MESH,
            ).wait_recv()

        return 0

    lax.fori_loop(0, NT // 2, drain_qg, 0)
    lax.fori_loop(1, NZ, drain_z, 0)
    lax.fori_loop(0, SLOTS, drain_dq, 0)
    lax.fori_loop(1, NT, drain_kv, 0)
    lax.fori_loop(1, NT, arrive_kv, 0)
    lax.fori_loop(0, NT, arrive_dq, 0)


def assemble(kv_tiles, dq_tiles, dq_out, dk_out, dv_out):
    t = lax.axis_index("tok")
    left = lax.broadcasted_iota(jnp.int32, (1, PAIR), 1) < HEAD
    first = (t // 2) % 2 == 0
    for p in range(NT // 2):
        cols = slice(p * PAIR, (p + 1) * PAIR)
        a = kv_tiles[2 * p].astype(F32)
        b = kv_tiles[2 * p + 1].astype(F32)
        dk_out[:, cols] = jnp.where(left, a, pltpu.roll(b, HEAD, 1)).astype(BF)
        dv_out[:, cols] = jnp.where(left, pltpu.roll(a, HEAD, 1), b).astype(BF)
        a = dq_tiles[2 * p].astype(F32)[0:SMALL]
        b = dq_tiles[2 * p + 1].astype(F32)[0:SMALL]
        a = jnp.where(first, a, pltpu.roll(a, HEAD, 1))
        b = jnp.where(first, pltpu.roll(b, HEAD, 1), b)
        dq_out[:, cols] = jnp.where(left, a, b).astype(BF)


def local(queries, keys, values, grad_out, lengths):
    dma = pltpu.SemaphoreType.DMA
    vm = pltpu.VMEM
    kv_tiles, dq_tiles = pl.pallas_call(
        kernel,
        out_shape=(
            jax.ShapeDtypeStruct((NT, OUT_KEYS, PAIR), BF),
            jax.ShapeDtypeStruct((NT, PAD, PAIR), BF),
        ),
        in_specs=[pl.BlockSpec(memory_space=pltpu.SMEM)]
        + [pl.BlockSpec(memory_space=pl.ANY)] * 4,
        out_specs=(pl.BlockSpec(memory_space=pl.ANY),) * 2,
        scratch_shapes=[
            vm((ROWS, NT * HEAD), BF), vm((ROWS, NT * HEAD), BF),
            vm((KEYS, PAIR), BF), vm((KEYS, PAIR), BF),
            vm((2, PAIR, ROWS), BF), vm((NT // 2, PAIR, ROWS), BF),
            vm((SLOTS, 2, PAIR, ROWS), BF),
            vm((2, KEYS, PAIR), BF), vm((2, 8, PAIR), F32),
            vm((BOTH, PAIR), BF), vm((BOTH, PAIR), BF),
            vm((HEAD, BOTH), BF), vm((PAIR, BOTH), BF),
            vm((BOTH, BLOCK), F32), vm((SLOTS, BOTH, BLOCK), BF), vm((SLOTS, BOTH, BLOCK), BF),
            vm((SLOTS, BLOCK, PAIR), BF), vm((SLOTS, BLOCK, PAIR), BF),
            vm((SLOTS, NZ, 2, BLOCK), F32), vm((SLOTS, 1, BLOCK), F32),
            vm((SLOTS, ROWS, PAIR), BF), vm((SLOTS, NZ, PIECE, PAIR), BF),
            vm((SLOTS, 2, PAD, PAIR), BF),
            vm((2, HALF, PAIR), F32), vm((2, HALF, PAIR), BF),
            vm((KEYS, PAIR), BF), vm((KEYS, PAIR), BF),
            dma((4,)), dma((NT // 2,)), dma((NT // 2,)), dma((2,)), dma((2,)),
            dma((SLOTS, NZ)), dma((SLOTS, NZ)), dma((SLOTS, NZ)), dma((SLOTS, NZ)),
            dma((2,)), dma((2,)), dma((NT,)), dma((NT,)),
            dma((SLOTS, 2, 2)), dma((NT,)), dma((2,)),
        ],
        compiler_params=pltpu.CompilerParams(
            collective_id=0, has_side_effects=True, vmem_limit_bytes=56 * 2**20
        ),
    )(lengths, queries, grad_out, keys, values)
    return pl.pallas_call(
        assemble,
        out_shape=(
            jax.ShapeDtypeStruct((SMALL, NT * HEAD), BF),
            jax.ShapeDtypeStruct((OUT_KEYS, NT * HEAD), BF),
            jax.ShapeDtypeStruct((OUT_KEYS, NT * HEAD), BF),
        ),
        in_specs=[pl.BlockSpec(memory_space=pltpu.VMEM)] * 2,
        out_specs=(pl.BlockSpec(memory_space=pltpu.VMEM),) * 3,
    )(kv_tiles, dq_tiles)


def solution(mesh):
    in_specs = (P("tok", None), P("view", None), P("view", None), P("tok", None), P("view"))
    out_specs = (P(("tok", "view"), None), P(("view", "tok"), None), P(("view", "tok"), None))
    return jax.shard_map(local, mesh=mesh, in_specs=in_specs, out_specs=out_specs, check_vma=False)
```

```python
import functools

import jax
import jax.numpy as jnp
from jax import lax
from jax.experimental import pallas as pl
from jax.experimental.pallas import tpu as pltpu
from jax.sharding import PartitionSpec as P

HEAD = 64
PAIR = 128
ROWS = 384
BLOCK = 2 * ROWS
KEYS = 1024
BOTH = 2 * KEYS
NZ = 8
NT = 16
SLOTS = 4
PIECE = ROWS // NZ
SMALL = PIECE // 2
OUT_KEYS = KEYS // NT
STEP1 = 512
LOG2E = 1.4426950408889634
STEP2 = 1024
HALF = 512
ROW = KEYS // 4
PAD = 32
MESH = pl.DeviceIdType.MESH
BF = jnp.bfloat16
F32 = jnp.float32
NN = (((1,), (0,)), ((), ()))


def mm(a, b):
    return lax.dot_general(a, b, NN, preferred_element_type=F32)


def kernel(
    len_ref, q_hbm, g_hbm, k_hbm, v_hbm,
    kv_tiles, dq_tiles,
    q_v, g_v, k_v, v_v, turned, qgt, qg_buf, kv_buf, len_buf,
    k0, v0, kt, vt1, s_ref, w_buf, ds_buf, cq_buf, cg_buf, stats, tops,
    dq_send, dq_recv, dq_fin, dkv, dkv_send, dkv_recv, dkv_fin,
    load_sem, qg_ssem, qg_rsem, kv_ssem, kv_rsem, st_ssem, st_rsem,
    dq_ssem, dq_rsem, x_ssem, x_rsem, kvf_ssem, kvf_rsem, dqf_ssem, dqf_rsem, self_sem,
):
    v = lax.axis_index("view")
    t = lax.axis_index("tok")
    z = v // 2
    core = v % 2
    y = t // 4
    par = (t + core) % 2
    other = 2 * z + 1 - core
    scale = HEAD ** -0.5

    pair_cols = pl.ds(pl.multiple_of(PAIR * (t // 2), PAIR), PAIR)
    loads = [
        pltpu.make_async_copy(q_hbm, q_v, load_sem.at[0]),
        pltpu.make_async_copy(g_hbm, g_v, load_sem.at[1]),
        pltpu.make_async_copy(k_hbm.at[:, pair_cols], k_v, load_sem.at[2]),
        pltpu.make_async_copy(v_hbm.at[:, pair_cols], v_v, load_sem.at[3]),
    ]
    for load in loads:
        load.start()

    barrier = pltpu.get_barrier_semaphore()

    def greet(view, tok):
        pl.semaphore_signal(barrier, inc=1, device_id=(view, tok), device_id_type=MESH)

    def greet_tok(d, _):
        greet(v, (t + d) % NT)
        return 0

    def greet_z(d, _):
        greet(2 * ((z + d) % NZ) + core, t)
        return 0

    def greet_other(d, _):
        tok = 2 * d + 1 - par

        @pl.when(tok != t)
        def _():
            greet(other, tok)

        return 0

    greet(other, t)
    lax.fori_loop(1, NT, greet_tok, 0)
    lax.fori_loop(0, NT // 2, greet_other, 0)
    lax.fori_loop(1, NZ, greet_z, 0)

    loads[0].wait()
    loads[1].wait()
    chosen = pl.ds(pl.multiple_of(HEAD * par, HEAD), HEAD)

    def row_at(i):
        i = jnp.int32(i)
        return i + jnp.where(i == 1, 1, 0) - jnp.where(i == 2, 1, 0)

    def pack(j, _):
        pair = 2 * ((y + row_at(j // 2)) % 4) + j % 2
        cols = pl.ds(pl.multiple_of(PAIR * pair, PAIR), PAIR)
        turned[0] = q_v[:, cols].T
        turned[1] = g_v[:, cols].T
        qgt[pair, 0:HEAD, :] = turned[0, chosen, :]
        qgt[pair, HEAD:PAIR, :] = turned[1, chosen, :]
        return 0


    lax.fori_loop(0, 2, pack, 0)
    pl.semaphore_wait(barrier, 1 + NT - 1 + NT // 2 - (1 - core) + NZ - 1)

    def qg_copy(pair):
        return pltpu.make_async_remote_copy(
            src_ref=qgt.at[pair], dst_ref=qg_buf.at[y, (t // 2) % 2],
            send_sem=qg_ssem.at[pair], recv_sem=qg_rsem.at[t // 2],
            device_id=(v, 2 * pair + par), device_id_type=MESH,
        )

    def send_row(j):
        for half in range(2):
            pair = 2 * ((y + row_at(j)) % 4) + half

            @pl.when(2 * pair + par != t)
            def _():
                qg_copy(pair).start()

            @pl.when(2 * pair + par == t)
            def _():
                qg_buf[y, half] = qgt[pair]

    send_row(0)
    lax.fori_loop(2, 4, pack, 0)
    send_row(1)

    length = len_ref[0]
    left = lax.broadcasted_iota(jnp.int32, (1, PAIR), 1) < HEAD
    row = lax.broadcasted_iota(jnp.int32, (KEYS, 1), 0)
    loads[2].wait()
    loads[3].wait()
    even = t % 2 == 0
    k_f = k_v[...].astype(F32)
    v_f = v_v[...].astype(F32)
    k_left = jnp.where(even, k_f, pltpu.roll(k_f, HEAD, 1))
    v_right = jnp.where(even, pltpu.roll(v_f, HEAD, 1), v_f)
    kv = jnp.where(left, k_left, v_right)
    kv = jnp.where(row < length, kv, kv[0:1, :])
    kv_buf[core] = kv.astype(BF)
    len_buf[core] = jnp.full((8, PAIR), length, jnp.int32).astype(F32)

    kv_copy = pltpu.make_async_remote_copy(
        src_ref=kv_buf.at[core], dst_ref=kv_buf.at[core],
        send_sem=kv_ssem.at[0], recv_sem=kv_rsem.at[0],
        device_id=(other, t), device_id_type=MESH,
    )
    len_copy = pltpu.make_async_remote_copy(
        src_ref=len_buf.at[core], dst_ref=len_buf.at[core],
        send_sem=kv_ssem.at[1], recv_sem=kv_rsem.at[1],
        device_id=(other, t), device_id_type=MESH,
    )
    kv_copy.start()
    len_copy.start()

    lax.fori_loop(4, NT // 2, pack, 0)

    col = lax.broadcasted_iota(jnp.int32, (1, KEYS), 1).astype(F32)
    sub = lax.broadcasted_iota(jnp.int32, (HEAD, 1), 0)

    def prepare(side):
        here = pl.ds(pl.multiple_of(KEYS * side, KEYS), KEYS)
        tile = kv_buf[side]
        f = tile.astype(F32)
        k0[here, :] = jnp.where(left, f, 0.0).astype(BF)
        v0[here, :] = jnp.where(left, 0.0, f).astype(BF)
        flipped = tile.T.astype(F32)
        okay = jnp.where(col < len_buf[side][0:1, 0:1], 1.0, 0.0)
        kt[:, here] = (flipped[0:HEAD] * okay).astype(BF)
        vt1[HEAD:PAIR, here] = (flipped[HEAD:PAIR] * okay).astype(BF)
        vt1[0:HEAD, here] = jnp.where(sub == 0, okay, 0.0).astype(BF)


    prepare(core)
    kv_copy.wait_recv()
    len_copy.wait_recv()
    prepare(1 - core)

    def stat_copy(i, to, frm):
        return pltpu.make_async_remote_copy(
            src_ref=stats.at[i, frm], dst_ref=stats.at[i, frm],
            send_sem=st_ssem.at[i, to], recv_sem=st_rsem.at[i, frm],
            device_id=(2 * to + core, t), device_id_type=MESH,
        )

    def dq_copy(i, to, frm):
        return pltpu.make_async_remote_copy(
            src_ref=dq_send.at[i, pl.ds(pl.multiple_of(PIECE * to, PIECE), PIECE), :],
            dst_ref=dq_recv.at[i, frm],
            send_sem=dq_ssem.at[i, to], recv_sem=dq_rsem.at[i, frm],
            device_id=(2 * to + core, t), device_id_type=MESH,
        )

    def far(d):
        return NZ // 2 + (d // 2) * (2 * ((d + 1) % 2) - 1)

    def block_of(i):
        return (y + 4 - row_at(i)) % 4

    def queries_of(i):
        sb = block_of(i)
        return jnp.concatenate([qg_buf[sb, 0], qg_buf[sb, 1]], axis=1)

    def scores_phase(i):
        sb = block_of(i)
        for half in range(2):
            source = 4 * sb + 2 * half + par

            @pl.when(source != t)
            def _():
                pltpu.make_async_remote_copy(
                    src_ref=qgt.at[0], dst_ref=qg_buf.at[sb, half],
                    send_sem=qg_ssem.at[0], recv_sem=qg_rsem.at[2 * sb + half],
                    device_id=(v, source), device_id_type=MESH,
                ).wait_recv()

        @pl.when(i < 2)
        def _():
            send_row(i + 2)

        qg = queries_of(i)
        top = jnp.full((8, BLOCK), -3e38, F32)
        for k in range(BOTH // STEP1):
            here = slice(k * STEP1, (k + 1) * STEP1)
            s = mm(k0[here, :], qg)
            s_ref[here, :] = s
            top = jnp.maximum(top, jnp.max(s.reshape(STEP1 // 8, 8, BLOCK), axis=0))
        top = jnp.max(top, axis=0, keepdims=True)
        for k in range(BOTH // STEP1):
            here = slice(k * STEP1, (k + 1) * STEP1)
            w_buf[i, here, :] = jnp.exp2((s_ref[here, :] - top) * (scale * LOG2E)).astype(BF)
        acc = mm(vt1[...], w_buf[i])
        total = acc[0:1, :]
        mean = jnp.sum(acc[HEAD:, :] * qg[HEAD:, :].astype(F32), axis=0, keepdims=True)
        top = top * scale
        tops[i] = top
        stats[i, z, 0:1, :] = top + jnp.log(total)
        stats[i, z, 1:2, :] = mean / total

        def send(d, _):
            stat_copy(i, (z + far(d)) % NZ, z).start()
            return 0

        lax.fori_loop(1, NZ, send, 0)

    def combine(i):
        def arrive(d, _):
            frm = (z + d) % NZ
            stat_copy(i, frm, frm).wait_recv()
            return 0

        lax.fori_loop(1, NZ, arrive, 0)
        logs = stats[i, :, 0, :]
        peak = jnp.max(logs, axis=0, keepdims=True)
        weight = jnp.exp(logs - peak)
        total = jnp.sum(weight, axis=0, keepdims=True)
        mean = jnp.sum(stats[i, :, 1, :] * weight, axis=0, keepdims=True) / total
        factor = jnp.exp(tops[i] - peak) / total
        qg = queries_of(i)
        scaled = (qg.astype(F32) * factor).T
        cq_buf[i] = jnp.where(left, scaled * scale, 0.0).astype(BF)
        cg_buf[i] = jnp.where(left, 0.0, scaled).astype(BF)
        return qg, mean, factor

    def give_dq(i, acc, factor):
        acc = acc * (factor * scale)
        two = jnp.concatenate([acc[:, :ROWS], acc[:, ROWS:]], axis=0)
        dq_send[i] = two.T.astype(BF)

        def send(d, _):
            dq_copy(i, (z + far(d)) % NZ, z).start()
            return 0

        lax.fori_loop(1, NZ, send, 0)

    def grads_phase(i):
        qg, mean, factor = combine(i)
        acc = jnp.zeros((HEAD, BLOCK), F32)
        for k in range(BOTH // STEP2):
            here = slice(k * STEP2, (k + 1) * STEP2)
            dp = mm(v0[here, :], qg)
            ds = (w_buf[i, here, :].astype(F32) * (dp - mean)).astype(BF)
            ds_buf[i, here, :] = ds
            acc = acc + mm(kt[:, here], ds)
        give_dq(i, acc, factor)

    def dq_give(i, half, c):
        return pltpu.make_async_remote_copy(
            src_ref=dq_fin.at[i, c], dst_ref=dq_tiles.at[t],
            send_sem=dqf_ssem.at[i, half, c], recv_sem=dqf_rsem.at[t],
            device_id=(2 * z + c, 4 * block_of(i) + 2 * half + par), device_id_type=MESH,
        )

    def own_piece(i, half, c):
        return jnp.logical_and(4 * block_of(i) + 2 * half + par == t, c == core)

    def reduce(i):
        def arrive(d, _):
            frm = (z + d) % NZ
            dq_copy(i, frm, frm).wait_recv()
            return 0

        lax.fori_loop(1, NZ, arrive, 0)
        piece = dq_send[i, pl.ds(pl.multiple_of(PIECE * z, PIECE), PIECE), :].astype(F32)

        def add(d, piece):
            return piece + dq_recv[i, (z + d) % NZ].astype(F32)

        piece = lax.fori_loop(1, NZ, add, piece)
        fill = jnp.zeros((PAD - SMALL, PAIR), F32)
        for c in range(2):
            rows = piece[c * SMALL : (c + 1) * SMALL, :]
            dq_fin[i, c] = jnp.concatenate([rows, fill], axis=0).astype(BF)
        for half in range(2):
            for c in range(2):
                @pl.when(jnp.logical_not(own_piece(i, half, c)))
                def _():
                    dq_give(i, half, c).start()

                @pl.when(own_piece(i, half, c))
                def _():
                    keep = pltpu.make_async_copy(dq_fin.at[i, c], dq_tiles.at[t], self_sem.at[0])
                    keep.start()
                    keep.wait()

    def kv_sum(here, blocks):
        acc = jnp.zeros((here.size, PAIR), F32)
        for i in blocks:
            acc = acc + mm(ds_buf[i, here, :], cq_buf[i]) + mm(w_buf[i, here, :], cg_buf[i])
        return acc

    def mate_rows(j):
        return pl.ds(pl.multiple_of(KEYS * (1 - core) + HALF * j, HALF), HALF)

    def turn(i, _):
        @pl.when(i < SLOTS)
        def _():
            scores_phase(i)

        @pl.when(i == SLOTS + 1)
        def _():
            for j in range(2):
                dkv[j] = kv_sum(mate_rows(j), (0, 1))

        @pl.when(i > 1)
        def _():
            grads_phase(i - 2)

        @pl.when(i > 3)
        def _():
            reduce(i - 4)

        return 0

    lax.fori_loop(0, SLOTS + 2, turn, 0)

    def dkv_copy(j):
        return pltpu.make_async_remote_copy(
            src_ref=dkv_send.at[j], dst_ref=dkv_recv.at[pl.ds(HALF * j, HALF), :],
            send_sem=x_ssem.at[j], recv_sem=x_rsem.at[j],
            device_id=(other, t), device_id_type=MESH,
        )

    def kv_out(to, frm):
        return pltpu.make_async_remote_copy(
            src_ref=dkv_fin.at[pl.ds(pl.multiple_of(OUT_KEYS * to, OUT_KEYS), OUT_KEYS), :],
            dst_ref=kv_tiles.at[frm],
            send_sem=kvf_ssem.at[to], recv_sem=kvf_rsem.at[frm],
            device_id=(v, to), device_id_type=MESH,
        )

    for j in range(2):
        dkv_send[j] = (dkv[j] + kv_sum(mate_rows(j), (2, 3))).astype(BF)
        dkv_copy(j).start()
    reduce(SLOTS - 2)
    kv_self = pltpu.make_async_copy(
        dkv_fin.at[pl.ds(pl.multiple_of(OUT_KEYS * t, OUT_KEYS), OUT_KEYS), :],
        kv_tiles.at[t], self_sem.at[1],
    )
    row_of = lax.broadcasted_iota(jnp.int32, (ROW, 1), 0)

    for j in range(4):
        to_y = (y + (2, 3, 1, 0)[j]) % 4
        start = pl.multiple_of(ROW * to_y, ROW)
        whole = kv_sum(pl.ds(pl.multiple_of(KEYS * core + start, ROW), ROW), range(SLOTS))
        if j == 0:
            dkv_copy(0).wait_recv()
            dkv_copy(1).wait_recv()
        rows = pl.ds(start, ROW)
        whole = whole + dkv_recv[rows, :].astype(F32)
        dkv_fin[rows, :] = jnp.where(row_of + start < length, whole, 0.0).astype(BF)
        for d in (2, 1, 3, 0):
            if j == 3 and d == 0:
                kv_self.start()
            else:
                kv_out(4 * to_y + (t + d) % 4, t).start()
    reduce(SLOTS - 1)

    kv_copy.wait_send()
    len_copy.wait_send()
    dkv_copy(0).wait_send()
    dkv_copy(1).wait_send()
    kv_self.wait()

    def drain_qg(pair, _):
        @pl.when(2 * pair + par != t)
        def _():
            qg_copy(pair).wait_send()

        return 0

    def drain_z(d, _):
        to = (z + d) % NZ
        for i in range(SLOTS):
            stat_copy(i, to, z).wait_send()
            dq_copy(i, to, z).wait_send()
        return 0

    def drain_dq(i, _):
        for half in range(2):
            for c in range(2):
                @pl.when(jnp.logical_not(own_piece(i, half, c)))
                def _():
                    dq_give(i, half, c).wait_send()

        return 0

    def drain_kv(d, _):
        kv_out((t + d) % NT, t).wait_send()
        return 0

    def arrive_kv(d, _):
        frm = (t + d) % NT
        kv_out(frm, frm).wait_recv()
        return 0

    def arrive_dq(frm, _):
        @pl.when(jnp.logical_or(frm != t, core == 1))
        def _():
            pltpu.make_async_remote_copy(
                src_ref=dq_fin.at[0, 0], dst_ref=dq_tiles.at[frm],
                send_sem=dqf_ssem.at[0, 0, 0], recv_sem=dqf_rsem.at[frm],
                device_id=(other, t), device_id_type=MESH,
            ).wait_recv()

        return 0

    lax.fori_loop(0, NT // 2, drain_qg, 0)
    lax.fori_loop(1, NZ, drain_z, 0)
    lax.fori_loop(0, SLOTS, drain_dq, 0)
    lax.fori_loop(1, NT, drain_kv, 0)
    lax.fori_loop(1, NT, arrive_kv, 0)
    lax.fori_loop(0, NT, arrive_dq, 0)


def assemble(kv_tiles, dq_tiles, dq_out, dk_out, dv_out):
    t = lax.axis_index("tok")
    left = lax.broadcasted_iota(jnp.int32, (1, PAIR), 1) < HEAD
    first = (t // 2) % 2 == 0
    for p in range(NT // 2):
        cols = slice(p * PAIR, (p + 1) * PAIR)
        a = kv_tiles[2 * p].astype(F32)
        b = kv_tiles[2 * p + 1].astype(F32)
        dk_out[:, cols] = jnp.where(left, a, pltpu.roll(b, HEAD, 1)).astype(BF)
        dv_out[:, cols] = jnp.where(left, pltpu.roll(a, HEAD, 1), b).astype(BF)
        a = dq_tiles[2 * p].astype(F32)[0:SMALL]
        b = dq_tiles[2 * p + 1].astype(F32)[0:SMALL]
        a = jnp.where(first, a, pltpu.roll(a, HEAD, 1))
        b = jnp.where(first, pltpu.roll(b, HEAD, 1), b)
        dq_out[:, cols] = jnp.where(left, a, b).astype(BF)


def local(queries, keys, values, grad_out, lengths):
    dma = pltpu.SemaphoreType.DMA
    vm = pltpu.VMEM
    kv_tiles, dq_tiles = pl.pallas_call(
        kernel,
        out_shape=(
            jax.ShapeDtypeStruct((NT, OUT_KEYS, PAIR), BF),
            jax.ShapeDtypeStruct((NT, PAD, PAIR), BF),
        ),
        in_specs=[pl.BlockSpec(memory_space=pltpu.SMEM)]
        + [pl.BlockSpec(memory_space=pl.ANY)] * 4,
        out_specs=(pl.BlockSpec(memory_space=pl.ANY),) * 2,
        scratch_shapes=[
            vm((ROWS, NT * HEAD), BF), vm((ROWS, NT * HEAD), BF),
            vm((KEYS, PAIR), BF), vm((KEYS, PAIR), BF),
            vm((2, PAIR, ROWS), BF), vm((NT // 2, PAIR, ROWS), BF),
            vm((SLOTS, 2, PAIR, ROWS), BF),
            vm((2, KEYS, PAIR), BF), vm((2, 8, PAIR), F32),
            vm((BOTH, PAIR), BF), vm((BOTH, PAIR), BF),
            vm((HEAD, BOTH), BF), vm((PAIR, BOTH), BF),
            vm((BOTH, BLOCK), F32), vm((SLOTS, BOTH, BLOCK), BF), vm((SLOTS, BOTH, BLOCK), BF),
            vm((SLOTS, BLOCK, PAIR), BF), vm((SLOTS, BLOCK, PAIR), BF),
            vm((SLOTS, NZ, 2, BLOCK), F32), vm((SLOTS, 1, BLOCK), F32),
            vm((SLOTS, ROWS, PAIR), BF), vm((SLOTS, NZ, PIECE, PAIR), BF),
            vm((SLOTS, 2, PAD, PAIR), BF),
            vm((2, HALF, PAIR), F32), vm((2, HALF, PAIR), BF),
            vm((KEYS, PAIR), BF), vm((KEYS, PAIR), BF),
            dma((4,)), dma((NT // 2,)), dma((NT // 2,)), dma((2,)), dma((2,)),
            dma((SLOTS, NZ)), dma((SLOTS, NZ)), dma((SLOTS, NZ)), dma((SLOTS, NZ)),
            dma((2,)), dma((2,)), dma((NT,)), dma((NT,)),
            dma((SLOTS, 2, 2)), dma((NT,)), dma((2,)),
        ],
        compiler_params=pltpu.CompilerParams(
            collective_id=0, has_side_effects=True, vmem_limit_bytes=56 * 2**20
        ),
    )(lengths, queries, grad_out, keys, values)
    return pl.pallas_call(
        assemble,
        out_shape=(
            jax.ShapeDtypeStruct((SMALL, NT * HEAD), BF),
            jax.ShapeDtypeStruct((OUT_KEYS, NT * HEAD), BF),
            jax.ShapeDtypeStruct((OUT_KEYS, NT * HEAD), BF),
        ),
        in_specs=[pl.BlockSpec(memory_space=pltpu.VMEM)] * 2,
        out_specs=(pl.BlockSpec(memory_space=pltpu.VMEM),) * 3,
    )(kv_tiles, dq_tiles)


def solution(mesh):
    in_specs = (P("tok", None), P("view", None), P("view", None), P("tok", None), P("view"))
    out_specs = (P(("tok", "view"), None), P(("view", "tok"), None), P(("view", "tok"), None))
    return jax.shard_map(local, mesh=mesh, in_specs=in_specs, out_specs=out_specs, check_vma=False)
```
